32 devices in a mesh: build: 8 (over z, y), prop: 4 (over x, core).
Axes of the slice: x: 2, y: 2, z: 4, core: 2. Of those that a mesh axis runs over, the one named last changes fastest.
Arguments:
- cholesky: bfloat16 [48, 2048, 2048], P(None, 'build'), may hold values from -0.09375 to 0.09375
- half_vectors: bfloat16 [48, 2048, 128], P(None, 'build'), may hold values from -0.00390625 to 0.00390625
- walkers: bfloat16 [32, 2048, 128], P(('build', 'prop')), may hold values from -6 to 6
- inverse_intersection: bfloat16 [32, 128, 128], P(('build', 'prop')), may hold values from -1.5 to 2.5
- fields: float32 [32, 48], replicated, may hold values from -6 to 6
- weights: float32 [32], replicated, may hold values from 0.5 to 2
- sources: int32 [32], replicated, may hold values from 0 to 31, as said below
Outputs:
- new_walkers: bfloat16 [32, 2048, 128], P(('build', 'prop'))
- new_weights: float32 [32], P(('build', 'prop'))
The draws below stay inside these ranges and needn't reach their ends.
Inputs may be any that keep to these rules, and one draw needn't show every extreme that they name: sources[w] has the same remainder modulo 4 as w; walkers 0 and 31 continue their own states.
All inputs are finite; a program needn't handle non-finite values.
Results may differ from the reference program's by a relative error of at most 0.014.
Values may be sent and summed in bfloat16 or wider, within the bound.
A program may use at most 192 MiB of HBM per device.

```python
import math
import jax
import jax.numpy as jnp
from jax import lax

ORB = 2048
NEL = 128
CHOL = 48
ORDER = 6
GROUPS = 4
PER_GROUP = 8
WALKERS = 32


def draw_sources(key, part):
    walker = jnp.arange(WALKERS, dtype=jnp.int32)
    picked = jax.random.randint(key, (WALKERS,), 0, PER_GROUP, dtype=jnp.int32)
    picked = jnp.where(walker == 0, 0, picked)
    picked = jnp.where(walker == WALKERS - 1, PER_GROUP - 1, picked)
    return picked * GROUPS + walker % GROUPS


def draw_inverse_intersection(key, part):
    noise = jax.random.normal(key, (WALKERS, NEL, NEL), jnp.float32)
    values = jnp.eye(NEL, dtype=jnp.float32)[None] + 0.5 * noise * NEL ** (-0.5)
    return jnp.clip(values, -1.5, 2.5).astype(jnp.bfloat16)


def steps_of(rng, dims, cuts, least, top_value):
    factor_of = 1.0
    for position, shards_of in cuts:
        heights = jax.random.uniform(jax.random.fold_in(jax.random.fold_in(rng, 6), position), (shards_of,), jnp.float32, least / len(cuts), top_value / len(cuts))
        factor_of = factor_of * jnp.repeat(jnp.exp(heights), dims[position] // shards_of).reshape((-1,) + (1,) * (len(dims) - 1 - position))
    return factor_of


def bell_draw(rng, extent, deviation, limit, cuts=(), held_as=jnp.bfloat16):
    array = deviation * jax.random.normal(rng, extent, jnp.float32)
    if cuts:
        array = array * steps_of(rng, extent, cuts, -0.22, 0.18)
    return jnp.clip(array, -limit, limit).astype(held_as)


def setup_inputs(seed: int = 0) -> dict:
    splits = jax.random.split(jax.random.key(seed), 8)
    return {
        "cholesky": bell_draw(splits[0], (CHOL, ORB, ORB), (2.0 * (CHOL * ORB) ** -0.5), 0.09375, ((1, 8),)),
        "half_vectors": bell_draw(splits[1], (CHOL, ORB, NEL), (0.15 * (ORB * NEL) ** -0.5), 0.00390625, ((1, 8),)),
        "walkers": bell_draw(splits[2], (WALKERS, ORB, NEL), 1.0, 6.0, ((0, 32),)),
        "inverse_intersection": draw_inverse_intersection(jax.random.fold_in(splits[7], 71), 0),
        "fields": bell_draw(splits[4], (WALKERS, CHOL), 1.0, 6.0, (), jnp.float32),
        "weights": jnp.clip(jnp.exp(jax.random.uniform(splits[5], (WALKERS,), jnp.float32, math.log(0.5), math.log(2.0))), 0.5, 2.0),
        "sources": draw_sources(jax.random.fold_in(splits[7], 71), 0),
    }


def reference(cholesky, half_vectors, walkers, inverse_intersection, fields, weights, sources):
    walker_count = walkers.shape[0]
    half_wide = half_vectors.astype(jnp.float32)

    def bias_of(walker_pair):
        walker_state, inverse = walker_pair
        theta_full = jnp.dot(walker_state, inverse, preferred_element_type=jnp.float32).astype(jnp.bfloat16)
        return jnp.einsum("gqi,qi->g", half_wide, theta_full.astype(jnp.float32))

    force_bias = lax.map(bias_of, (walkers, inverse_intersection))
    exponent = jnp.sum(force_bias * (fields - 0.5 * force_bias), axis=-1)
    grown_weights = weights * jnp.exp(exponent)
    overall = jnp.sum(grown_weights)
    new_weights = jnp.take(grown_weights, sources, axis=0) * walker_count / overall
    coeffs = (fields - force_bias).astype(jnp.bfloat16)
    flat_vectors = cholesky.reshape(CHOL, ORB * ORB)

    def propagate(walker):
        source = lax.dynamic_index_in_dim(sources, walker, 0, False).astype(jnp.int32)
        coeff_row = lax.dynamic_slice_in_dim(coeffs, source, 1, 0)
        potential = jnp.dot(coeff_row, flat_vectors, preferred_element_type=jnp.float32)
        potential = potential.astype(jnp.bfloat16).reshape(ORB, ORB)
        begin_state = lax.dynamic_index_in_dim(walkers, source, 0, False)
        summed = begin_state.astype(jnp.float32)
        current = begin_state
        for degree in range(1, ORDER + 1):
            product = jnp.dot(potential, current, preferred_element_type=jnp.float32) / degree
            summed = summed + product
            current = product.astype(jnp.bfloat16)
        return summed.astype(jnp.bfloat16)

    new_walkers = lax.map(propagate, jnp.arange(walker_count, dtype=jnp.int32))
    return new_walkers, new_weights
```

```python
import functools

import jax
import jax.numpy as jnp
from jax import lax
from jax.experimental import pallas as pl
from jax.experimental.pallas import tpu as pltpu
from jax.sharding import PartitionSpec as P

ORDER = 6
TILE = 16
SLOTS = 4
MESH = pl.DeviceIdType.MESH
f32 = jnp.float32
bf16 = jnp.bfloat16


def spread(coeffs, vectors):
    count = coeffs.shape[0]
    wide = vectors * TILE
    lane = lax.broadcasted_iota(jnp.int32, (vectors, wide), 1) // TILE
    row = lax.broadcasted_iota(jnp.int32, (vectors, wide), 0)
    repeat_columns = (lane == row).astype(f32).astype(bf16)
    line = lax.broadcasted_iota(jnp.int32, (count * TILE, count), 0) // TILE
    walker = lax.broadcasted_iota(jnp.int32, (count * TILE, count), 1)
    repeat_rows = (line == walker).astype(f32).astype(bf16)
    along = jnp.dot(coeffs, repeat_columns, preferred_element_type=f32).astype(bf16)
    both = jnp.dot(repeat_rows, along, preferred_element_type=f32)
    at_row = lax.broadcasted_iota(jnp.int32, (count * TILE, wide), 0) % TILE
    at_lane = lax.broadcasted_iota(jnp.int32, (count * TILE, wide), 1) % TILE
    return jnp.where(at_row == at_lane, both, 0.0).astype(bf16)


def step_kernel(
    nb,
    picked_ref,
    starts_ref,
    chol_ref,
    out_ref,
    chunks,
    mixer,
    tiles,
    pot,
    terms,
    summed,
    finals,
    landed,
    load_sem,
    self_sem,
    pot_send,
    pot_recv,
    state_send,
    state_recv,
    term_send,
    term_recv,
    last_send,
    last_recv,
):
    me = lax.axis_index("build")
    nh = nb // 2
    half = me // nh
    place = lax.rem(me, nh)
    peer = lax.rem(me + nh, nb)
    vectors, br, orbitals = chol_ref.shape
    hr = orbitals // 2
    row_tiles = br // TILE
    group = min(nb, 8)
    cols = min(orbitals, 512)
    rows = min(hr, 256)

    def load(t):
        slot = lax.rem(t, SLOTS)
        return pltpu.make_async_copy(
            chol_ref.at[:, pl.ds(t * TILE, TILE), :], chunks.at[slot], load_sem.at[slot]
        )

    for t in range(min(SLOTS - 1, row_tiles)):
        load(jnp.int32(t)).start()

    barrier = pltpu.get_barrier_semaphore()

    def greet(j, carry):
        pl.semaphore_signal(
            barrier, inc=1, device_id={"build": lax.rem(me + j, nb)}, device_id_type=MESH
        )
        return carry

    lax.fori_loop(1, nb, greet, 0)

    def fill(v, carry):
        c = picked_ref[pl.ds(v * group, group), :]
        mixer[pl.ds(v * group * TILE, group * TILE), :] = spread(c, vectors)
        return carry

    lax.fori_loop(0, nb // group, fill, 0)
    own_rows = pl.ds(me * br, br)
    for s in range(2):
        terms[0, s, own_rows, :] = starts_ref[place + s * nh]
    pl.semaphore_wait(barrier, nb - 1)

    def send_pot(s, j, first, count):
        to = lax.rem(place + j, nh)
        return pltpu.make_async_remote_copy(
            src_ref=tiles.at[to + s * nh, pl.ds(first, count)],
            dst_ref=pot.at[s, pl.ds(place * br + first, count)],
            send_sem=pot_send.at[s],
            recv_sem=pot_recv.at[s],
            device_id={"build": half * nh + to},
            device_id_type=MESH,
        )

    def send_state(s, j):
        to = lax.rem(me + j, nb)
        return pltpu.make_async_remote_copy(
            src_ref=starts_ref.at[lax.rem(to, nh) + s * nh],
            dst_ref=terms.at[0, s, own_rows],
            send_sem=state_send.at[s],
            recv_sem=state_recv.at[s],
            device_id={"build": to},
            device_id_type=MESH,
        )

    def block(t, carry):
        slot = lax.rem(t, SLOTS)

        @pl.when(t + SLOTS - 1 < row_tiles)
        def _():
            load(t + SLOTS - 1).start()

        load(t).wait()

        def part(i, inner):
            v = i // (orbitals // cols)
            c = lax.rem(i, orbitals // cols) * cols
            c = pl.multiple_of(c, cols)
            right = chunks[slot, :, :, pl.ds(c, cols)].reshape(vectors * TILE, cols)
            left = mixer[pl.ds(v * group * TILE, group * TILE), :]
            made = jnp.dot(left, right, preferred_element_type=f32).astype(bf16)
            tiles[pl.ds(v * group, group), pl.ds(t * TILE, TILE), pl.ds(c, cols)] = (
                made.reshape(group, TILE, cols)
            )
            return inner

        lax.fori_loop(0, (nb // group) * (orbitals // cols), part, 0)

        def push(j, inner):
            send_pot(0, j, t * TILE, TILE).start()
            return inner

        lax.fori_loop(1, nh, push, 0)
        return carry

    lax.fori_loop(0, row_tiles, block, 0)

    for s in range(2):

        def push_state(j, carry):
            send_state(s, j).start()
            return carry

        lax.fori_loop(1, nb, push_state, 0)

    def keep(s):
        return pltpu.make_async_copy(
            tiles.at[place + s * nh], pot.at[s, pl.ds(place * br, br)], self_sem.at[s]
        )

    for s in range(2):
        keep(s).start()

    def others(ref, sem, count):
        return pltpu.make_async_copy(ref.at[pl.ds(0, count)], ref.at[pl.ds(0, count)], sem)

    far = (nh - 1) * br
    others(pot.at[0], pot_send.at[0], far).wait()

    def push_rest(j, carry):
        send_pot(1, j, 0, br).start()
        return carry

    lax.fori_loop(1, nh, push_rest, 0)

    def send_term(k, s, first):
        at = pl.ds(half * hr + first, rows)
        return pltpu.make_async_remote_copy(
            src_ref=terms.at[k, s, at],
            dst_ref=terms.at[k, s, at],
            send_sem=term_send.at[k, s],
            recv_sem=term_recv.at[k, s],
            device_id={"build": peer},
            device_id_type=MESH,
        )

    def send_last(s, first):
        return pltpu.make_async_remote_copy(
            src_ref=finals.at[s, pl.ds(first, rows)],
            dst_ref=landed.at[pl.ds(first, rows)],
            send_sem=last_send,
            recv_sem=last_recv,
            device_id={"build": peer},
            device_id_type=MESH,
        )

    def advance(k, s):
        if k == 1:
            others(terms.at[0, s], state_recv.at[s], (nb - 1) * br).wait()
            keep(s).wait()
            others(pot.at[s], pot_recv.at[s], far).wait()
        else:
            others(terms.at[k - 1, s], term_recv.at[k - 1, s], hr).wait()

        def piece(i, carry):
            first = pl.multiple_of(i * rows, rows)
            at = pl.ds(first, rows)
            here = pl.ds(pl.multiple_of(half * hr + first, rows), rows)
            product = jnp.dot(pot[s, at, :], terms[k - 1, s], preferred_element_type=f32) / k
            if k == 1:
                total = terms[0, s, here, :].astype(f32) + product
            else:
                total = summed[s, at, :] + product
            if k < ORDER:
                summed[s, at, :] = total
                terms[k, s, here, :] = product.astype(bf16)
                send_term(k, s, first).start()
            else:
                finals[s, at, :] = total.astype(bf16)

                @pl.when(half != s)
                def _():
                    send_last(s, first).start()

            return carry

        lax.fori_loop(0, hr // rows, piece, 0)

    lead = 3
    for k in range(1, lead + 1):
        advance(k, 0)
    for k in range(1, ORDER + 1):
        advance(k, 1)
        if k + lead <= ORDER:
            advance(k + lead, 0)

    own_half = pl.ds(pl.multiple_of(half * hr, hr), hr)
    out_ref[own_half, :] = finals[half]
    others(landed, last_recv, hr).wait()
    other_half = pl.ds(pl.multiple_of((1 - half) * hr, hr), hr)
    out_ref[other_half, :] = landed[...]
    others(landed, last_send, hr).wait()
    others(pot.at[1], pot_send.at[1], far).wait()
    for s in range(2):
        others(terms.at[0, s], state_send.at[s], (nb - 1) * br).wait()
        for k in range(1, ORDER):
            others(terms.at[k, s], term_send.at[k, s], hr).wait()


def propagate(nb, picked, starts, cholesky):
    vectors, br, orbitals = cholesky.shape
    electrons = starts.shape[2]
    hr = orbitals // 2
    vmem = pl.BlockSpec(memory_space=pltpu.VMEM)
    return pl.pallas_call(
        functools.partial(step_kernel, nb),
        out_shape=jax.ShapeDtypeStruct((orbitals, electrons), bf16),
        in_specs=[vmem, vmem, pl.BlockSpec(memory_space=pl.ANY)],
        out_specs=vmem,
        scratch_shapes=[
            pltpu.VMEM((SLOTS, vectors, TILE, orbitals), bf16),
            pltpu.VMEM((nb * TILE, vectors * TILE), bf16),
            pltpu.VMEM((nb, br, orbitals), bf16),
            pltpu.VMEM((2, hr, orbitals), bf16),
            pltpu.VMEM((ORDER, 2, orbitals, electrons), bf16),
            pltpu.VMEM((2, hr, electrons), f32),
            pltpu.VMEM((2, hr, electrons), bf16),
            pltpu.VMEM((hr, electrons), bf16),
            pltpu.SemaphoreType.DMA((SLOTS,)),
            pltpu.SemaphoreType.DMA((2,)),
            pltpu.SemaphoreType.DMA((2,)),
            pltpu.SemaphoreType.DMA((2,)),
            pltpu.SemaphoreType.DMA((2,)),
            pltpu.SemaphoreType.DMA((2,)),
            pltpu.SemaphoreType.DMA((ORDER, 2)),
            pltpu.SemaphoreType.DMA((ORDER, 2)),
            pltpu.SemaphoreType.DMA,
            pltpu.SemaphoreType.DMA,
        ],
        compiler_params=pltpu.CompilerParams(
            collective_id=0, has_side_effects=True, vmem_limit_bytes=56 * 1024 * 1024
        ),
    )(picked, starts, cholesky)


def factors(force_bias, chosen_fields, chosen_weights):
    exponent = jnp.sum(force_bias * (chosen_fields - 0.5 * force_bias), axis=-1)
    return chosen_weights * jnp.exp(exponent)


def shards(cholesky, half_vectors, walkers, inverse_intersection, fields, weights, sources):
    build_count = lax.axis_size("build")
    prop_count = lax.axis_size("prop")
    builder = lax.axis_index("build")
    member = lax.axis_index("prop")
    orbitals = walkers.shape[1]
    electrons = walkers.shape[2]
    vectors = cholesky.shape[0]
    block_rows = orbitals // build_count
    own_state = walkers[0]
    theta_full = jnp.dot(
        own_state, inverse_intersection[0], preferred_element_type=jnp.float32
    ).astype(jnp.bfloat16)
    outgoing = (
        theta_full.reshape(1, build_count, block_rows, electrons),
        own_state.reshape(1, build_count, block_rows, electrons),
    )
    got_theta, got_state = (
        lax.all_to_all(outgoing[0], "build", split_axis=1, concat_axis=0, tiled=True),
        lax.all_to_all(outgoing[1], "build", split_axis=1, concat_axis=0, tiled=True),
    )
    partial_value = jnp.einsum(
        "wri,gri->wg", got_theta[:, 0], half_vectors, preferred_element_type=jnp.float32
    )
    force_bias = lax.psum(partial_value, "build")
    group_fields = lax.dynamic_index_in_dim(
        fields.reshape(build_count, prop_count, vectors), member, 1, False
    )
    group_weights = lax.dynamic_index_in_dim(
        weights.reshape(build_count, prop_count), member, 1, False
    )
    group_sources = (
        lax.dynamic_index_in_dim(sources.reshape(build_count, prop_count), member, 1, False)
        // prop_count
    )
    grown_weights = factors(force_bias, group_fields, group_weights)
    overall = lax.psum(jnp.sum(grown_weights), "prop")
    coeffs = (group_fields - force_bias).astype(jnp.bfloat16)
    picked = jnp.take(coeffs, group_sources, axis=0)
    starts = jnp.take(got_state[:, 0], group_sources, axis=0)
    stepped = propagate(build_count, picked, starts, cholesky)
    own_source = lax.dynamic_index_in_dim(group_sources, builder, 0, False)
    kept_weight = lax.dynamic_index_in_dim(grown_weights, own_source, 0, False)
    new_weight = kept_weight * (build_count * prop_count) / overall
    return (stepped[None], new_weight.reshape(1))


def solution(mesh):
    placed = (
        P(None, "build", None),
        P(None, "build", None),
        P(("build", "prop"), None, None),
        P(("build", "prop"), None, None),
        P(),
        P(),
        P(),
    )
    return jax.shard_map(
        shards,
        mesh=mesh,
        in_specs=placed,
        out_specs=(P(("build", "prop"), None, None), P(("build", "prop"))),
        check_vma=False,
    )
```

```python
import functools

import jax
import jax.numpy as jnp
from jax import lax
from jax.experimental import pallas as pl
from jax.experimental.pallas import tpu as pltpu
from jax.sharding import PartitionSpec as P

ORDER = 6
TILE = 16
SLOTS = 4
MESH = pl.DeviceIdType.MESH
f32 = jnp.float32
bf16 = jnp.bfloat16


def spread(coeffs, wide):
    count, vectors = coeffs.shape
    lane = lax.broadcasted_iota(jnp.int32, (vectors, wide), 1) // TILE
    row = lax.broadcasted_iota(jnp.int32, (vectors, wide), 0)
    repeat_columns = (lane == row).astype(f32).astype(bf16)
    line = lax.broadcasted_iota(jnp.int32, (count * TILE, count), 0) // TILE
    walker = lax.broadcasted_iota(jnp.int32, (count * TILE, count), 1)
    repeat_rows = (line == walker).astype(f32).astype(bf16)
    along = jnp.dot(coeffs, repeat_columns, preferred_element_type=f32).astype(bf16)
    both = jnp.dot(repeat_rows, along, preferred_element_type=f32)
    at_row = lax.broadcasted_iota(jnp.int32, (count * TILE, wide), 0) % TILE
    at_lane = lax.broadcasted_iota(jnp.int32, (count * TILE, wide), 1) % TILE
    return jnp.where(at_row == at_lane, both, 0.0).astype(bf16)


def step_kernel(
    nb,
    npr,
    walker_ref,
    inverse_ref,
    half_ref,
    fields_ref,
    weights_ref,
    choice_ref,
    origin_ref,
    chol_ref,
    out_ref,
    grown_ref,
    overall_ref,
    got,
    inverses,
    theta,
    mixed,
    parts,
    sums,
    picked_ref,
    starts_ref,
    chunks,
    mixer,
    tiles,
    pot,
    terms,
    summed,
    finals,
    landed,
    load_sem,
    self_sem,
    got_send,
    got_recv,
    inverse_send,
    inverse_recv,
    part_send,
    part_recv,
    sum_send,
    sum_recv,
    pot_send,
    pot_recv,
    state_send,
    state_recv,
    term_send,
    term_recv,
    last_send,
    last_recv,
):
    me = lax.axis_index("build")
    mine = lax.axis_index("prop")
    nh = nb // 2
    half = me // nh
    place = lax.rem(me, nh)
    peer = lax.rem(me + nh, nb)
    vectors, br, orbitals = chol_ref.shape
    electrons = walker_ref.shape[1]
    wide = vectors * TILE
    lanes = fields_ref.shape[1]
    hr = orbitals // 2
    row_tiles = br // TILE
    slots = chunks.shape[0]
    group = min(nb, 8)
    cols = min(orbitals, 512)
    rows = min(hr, 512)
    pieces = min(4, row_tiles)

    def load(t):
        slot = lax.rem(t, slots)
        return pltpu.make_async_copy(
            chol_ref.at[:, pl.ds(t * TILE, TILE), :], chunks.at[slot], load_sem.at[slot]
        )

    def others(ref, sem, count):
        return pltpu.make_async_copy(ref.at[pl.ds(0, count)], ref.at[pl.ds(0, count)], sem)

    barrier = pltpu.get_barrier_semaphore()

    def greet(j, carry):
        pl.semaphore_signal(
            barrier, inc=1, device_id={"build": lax.rem(me + j, nb)}, device_id_type=MESH
        )
        return carry

    lax.fori_loop(1, nb, greet, 0)
    for j in range(1, npr):
        pl.semaphore_signal(
            barrier, inc=1, device_id={"prop": lax.rem(mine + j, npr)}, device_id_type=MESH
        )
    for t in range(min(slots, row_tiles)):
        load(jnp.int32(t)).start()
    own_rows = pl.ds(pl.multiple_of(me * br, br), br)
    got[me] = walker_ref[own_rows, :]
    inverses[me] = inverse_ref[...]
    pl.semaphore_wait(barrier, nb - 1 + npr - 1)

    def share(j, carry):
        to = lax.rem(me + j, nb)
        pltpu.make_async_remote_copy(
            src_ref=inverse_ref,
            dst_ref=inverses.at[me],
            send_sem=inverse_send,
            recv_sem=inverse_recv,
            device_id={"build": to},
            device_id_type=MESH,
        ).start()
        pltpu.make_async_remote_copy(
            src_ref=walker_ref.at[pl.ds(to * br, br)],
            dst_ref=got.at[me],
            send_sem=got_send,
            recv_sem=got_recv,
            device_id={"build": to},
            device_id_type=MESH,
        ).start()
        return carry

    lax.fori_loop(1, nb, share, 0)
    others(inverses, inverse_recv, nb - 1).wait()
    others(got, got_recv, nb - 1).wait()

    def rotate(v, carry):
        theta[v] = jnp.dot(got[v], inverses[v], preferred_element_type=f32).astype(bf16)
        starts_ref[v] = got[origin_ref[v]]
        return carry

    lax.fori_loop(0, nb, rotate, 0)

    def bias(u, carry):
        first = pl.multiple_of(u * group, group)
        mixed[...] = jnp.zeros_like(mixed)

        def add(t, inner):
            at = pl.ds(pl.multiple_of(t * TILE, TILE), TILE)
            left = theta[pl.ds(first, group), at, :].reshape(group * TILE, electrons)
            right = half_ref[:, at, :].reshape(wide, electrons)
            mixed[...] += lax.dot_general(
                left, right, (((1,), (1,)), ((), ())), preferred_element_type=f32
            )
            return inner

        lax.fori_loop(0, row_tiles, add, 0)
        at_row = lax.broadcasted_iota(jnp.int32, (group * TILE, wide), 0) % TILE
        at_lane = lax.broadcasted_iota(jnp.int32, (group * TILE, wide), 1) % TILE
        kept = jnp.where(at_row == at_lane, mixed[...], 0.0)
        short = jnp.sum(kept.reshape(group, TILE, wide), axis=1)
        source = lax.broadcasted_iota(jnp.int32, (wide, lanes), 0) // TILE
        target = lax.broadcasted_iota(jnp.int32, (wide, lanes), 1)
        gather = (source == target).astype(f32)
        parts[me, pl.ds(first, group), :] = jnp.dot(
            short, gather, precision=lax.Precision.HIGHEST, preferred_element_type=f32
        )
        return carry

    lax.fori_loop(0, nb // group, bias, 0)

    def tell(j, carry):
        pltpu.make_async_remote_copy(
            src_ref=parts.at[me],
            dst_ref=parts.at[me],
            send_sem=part_send,
            recv_sem=part_recv,
            device_id={"build": lax.rem(me + j, nb)},
            device_id_type=MESH,
        ).start()
        return carry

    lax.fori_loop(1, nb, tell, 0)

    def send_state(s, j):
        to = lax.rem(me + j, nb)
        return pltpu.make_async_remote_copy(
            src_ref=starts_ref.at[lax.rem(to, nh) + s * nh],
            dst_ref=terms.at[0, s, own_rows],
            send_sem=state_send.at[s],
            recv_sem=state_recv.at[s],
            device_id={"build": to},
            device_id_type=MESH,
        )

    def push_states(s):
        def push_state(j, carry):
            send_state(s, j).start()
            return carry

        lax.fori_loop(1, nb, push_state, 0)

    push_states(0)
    for s in range(2):
        terms[0, s, own_rows, :] = starts_ref[place + s * nh]
    others(parts, part_recv, nb - 1).wait()
    force_bias = lax.fori_loop(
        1, nb, lambda j, held: held + parts[j], parts[0]
    )
    drawn = fields_ref[...]
    exponent = jnp.sum(force_bias * (drawn - 0.5 * force_bias), axis=-1, keepdims=True)
    grown = weights_ref[...] * jnp.exp(exponent)
    grown_ref[...] = grown
    sums[mine] = jnp.broadcast_to(jnp.sum(grown, axis=0, keepdims=True), sums.shape[1:])
    for j in range(1, npr):
        pltpu.make_async_remote_copy(
            src_ref=sums.at[mine],
            dst_ref=sums.at[mine],
            send_sem=sum_send,
            recv_sem=sum_recv,
            device_id={"prop": lax.rem(mine + j, npr)},
            device_id_type=MESH,
        ).start()
    coeffs = (drawn - force_bias).astype(bf16)
    picked_ref[...] = jnp.dot(choice_ref[...], coeffs, preferred_element_type=f32)

    def fill(v, carry):
        c = picked_ref[pl.ds(pl.multiple_of(v * group, group), group), :].astype(bf16)
        at = pl.ds(pl.multiple_of(v * group * TILE, group * TILE), group * TILE)
        mixer[at, :] = spread(c, wide)
        return carry

    if nb == group:
        mixer[...] = spread(picked_ref[...].astype(bf16), wide)
    else:
        lax.fori_loop(0, nb // group, fill, 0)

    def send_pot(s, j, first, count):
        to = lax.rem(place + j, nh)
        return pltpu.make_async_remote_copy(
            src_ref=tiles.at[to + s * nh, pl.ds(first, count)],
            dst_ref=pot.at[s, pl.ds(place * br + first, count)],
            send_sem=pot_send.at[s],
            recv_sem=pot_recv.at[s],
            device_id={"build": half * nh + to},
            device_id_type=MESH,
        )

    def block(t, carry):
        slot = lax.rem(t, slots)
        load(t).wait()

        def part(i, inner):
            v = i // (orbitals // cols)
            c = lax.rem(i, orbitals // cols) * cols
            c = pl.multiple_of(c, cols)
            right = chunks[slot, :, :, pl.ds(c, cols)].reshape(vectors * TILE, cols)
            left = mixer[pl.ds(pl.multiple_of(v * group * TILE, group * TILE), group * TILE), :]
            made = jnp.dot(left, right, preferred_element_type=f32).astype(bf16)
            tiles[pl.ds(v * group, group), pl.ds(pl.multiple_of(t * TILE, TILE), TILE), pl.ds(c, cols)] = (
                made.reshape(group, TILE, cols)
            )
            return inner

        lax.fori_loop(0, (nb // group) * (orbitals // cols), part, 0)

        @pl.when(t + slots < row_tiles)
        def _():
            load(t + slots).start()

        def push(j, inner):
            send_pot(0, j, t * TILE, TILE).start()
            return inner

        lax.fori_loop(1, nh, push, 0)
        return carry

    lax.fori_loop(0, row_tiles, block, 0)

    push_states(1)

    def keep(s):
        return pltpu.make_async_copy(
            tiles.at[place + s * nh], pot.at[s, pl.ds(place * br, br)], self_sem.at[s]
        )

    for s in range(2):
        keep(s).start()

    far = (nh - 1) * br

    def push_rest(piece):
        count = br // pieces

        def push_one(j, carry):
            send_pot(1, j, piece * count, count).start()
            return carry

        lax.fori_loop(1, nh, push_one, 0)

    def send_term(k, s, first):
        at = pl.ds(half * hr + first, rows)
        return pltpu.make_async_remote_copy(
            src_ref=terms.at[k, s, at],
            dst_ref=terms.at[k, s, at],
            send_sem=term_send.at[k, s],
            recv_sem=term_recv.at[k, s],
            device_id={"build": peer},
            device_id_type=MESH,
        )

    def send_last(s, first):
        return pltpu.make_async_remote_copy(
            src_ref=finals.at[s, pl.ds(first, rows)],
            dst_ref=landed.at[pl.ds(first, rows)],
            send_sem=last_send,
            recv_sem=last_recv,
            device_id={"build": peer},
            device_id_type=MESH,
        )

    def advance(k, s):
        if k == 1:
            others(terms.at[0, s], state_recv.at[s], (nb - 1) * br).wait()
            keep(s).wait()
            others(pot.at[s], pot_recv.at[s], far).wait()
        else:
            others(terms.at[k - 1, s], term_recv.at[k - 1, s], hr).wait()

        def piece(i, carry):
            first = pl.multiple_of(i * rows, rows)
            at = pl.ds(first, rows)
            here = pl.ds(pl.multiple_of(half * hr + first, rows), rows)
            product = jnp.dot(pot[s, at, :], terms[k - 1, s], preferred_element_type=f32) / k
            if k == 1:
                total = terms[0, s, here, :].astype(f32) + product
            else:
                total = summed[s, at, :] + product
            if k < ORDER:
                summed[s, at, :] = total
                terms[k, s, here, :] = product.astype(bf16)
                send_term(k, s, first).start()
            else:
                finals[s, at, :] = total.astype(bf16)

                @pl.when(half != s)
                def _():
                    send_last(s, first).start()

            return carry

        lax.fori_loop(0, hr // rows, piece, 0)

    lead = 3
    push_rest(0)
    for k in range(1, lead + 1):
        advance(k, 0)
        if k < pieces:
            push_rest(k)
    for k in range(1, ORDER + 1):
        advance(k, 1)
        if k + lead <= ORDER:
            advance(k + lead, 0)

    own_half = pl.ds(pl.multiple_of(half * hr, hr), hr)
    out_ref[own_half, :] = finals[half]
    others(landed, last_recv, hr).wait()
    other_half = pl.ds(pl.multiple_of((1 - half) * hr, hr), hr)
    out_ref[other_half, :] = landed[...]
    others(landed, last_send, hr).wait()
    others(sums, sum_recv, npr - 1).wait()
    overall_ref[...] = jnp.sum(sums[...], axis=0)
    others(sums, sum_send, npr - 1).wait()
    others(inverses, inverse_send, nb - 1).wait()
    others(got, got_send, nb - 1).wait()
    others(parts, part_send, nb - 1).wait()
    for s in range(2):
        others(pot.at[s], pot_send.at[s], far).wait()
        others(terms.at[0, s], state_send.at[s], (nb - 1) * br).wait()
        for k in range(1, ORDER):
            others(terms.at[k, s], term_send.at[k, s], hr).wait()


def shards(cholesky, half_vectors, walkers, inverse_intersection, fields, weights, sources):
    nb = lax.axis_size("build")
    npr = lax.axis_size("prop")
    builder = lax.axis_index("build")
    member = lax.axis_index("prop")
    vectors, br, orbitals = cholesky.shape
    electrons = walkers.shape[2]
    hr = orbitals // 2
    wide = vectors * TILE
    lanes = -(-vectors // 128) * 128
    group = min(nb, 8)
    slots = min(SLOTS, br // TILE)
    group_fields = lax.dynamic_index_in_dim(fields.reshape(nb, npr, vectors), member, 1, False)
    group_fields = jnp.pad(group_fields, ((0, 0), (0, lanes - vectors)))
    group_weights = lax.dynamic_index_in_dim(weights.reshape(nb, npr), member, 1, False)
    origin = lax.dynamic_index_in_dim(sources.reshape(nb, npr), member, 1, False) // npr
    choice = (origin[:, None] == jnp.arange(nb, dtype=origin.dtype)[None, :]).astype(bf16)
    vmem = pl.BlockSpec(memory_space=pltpu.VMEM)
    dma = pltpu.SemaphoreType.DMA
    stepped, grown, overall = pl.pallas_call(
        functools.partial(step_kernel, nb, npr),
        out_shape=(
            jax.ShapeDtypeStruct((orbitals, electrons), bf16),
            jax.ShapeDtypeStruct((nb, 1), f32),
            jax.ShapeDtypeStruct((8, 128), f32),
        ),
        in_specs=[vmem] * 6
        + [pl.BlockSpec(memory_space=pltpu.SMEM), pl.BlockSpec(memory_space=pl.ANY)],
        out_specs=(vmem, vmem, vmem),
        scratch_shapes=[
            pltpu.VMEM((nb, br, electrons), bf16),
            pltpu.VMEM((nb,) + inverse_intersection.shape[1:], bf16),
            pltpu.VMEM((nb, br, electrons), bf16),
            pltpu.VMEM((group * TILE, wide), f32),
            pltpu.VMEM((nb, nb, lanes), f32),
            pltpu.VMEM((npr, 8, 128), f32),
            pltpu.VMEM((nb, lanes), f32),
            pltpu.VMEM((nb, br, electrons), bf16),
            pltpu.VMEM((slots, vectors, TILE, orbitals), bf16),
            pltpu.VMEM((nb * TILE, wide), bf16),
            pltpu.VMEM((nb, br, orbitals), bf16),
            pltpu.VMEM((2, hr, orbitals), bf16),
            pltpu.VMEM((ORDER, 2, orbitals, electrons), bf16),
            pltpu.VMEM((2, hr, electrons), f32),
            pltpu.VMEM((2, hr, electrons), bf16),
            pltpu.VMEM((hr, electrons), bf16),
            dma((slots,)),
            dma((2,)),
            dma,
            dma,
            dma,
            dma,
            dma,
            dma,
            dma,
            dma,
            dma((2,)),
            dma((2,)),
            dma((2,)),
            dma((2,)),
            dma((ORDER, 2)),
            dma((ORDER, 2)),
            dma,
            dma,
        ],
        compiler_params=pltpu.CompilerParams(
            collective_id=0, has_side_effects=True, vmem_limit_bytes=60 * 1024 * 1024
        ),
    )(
        walkers[0],
        inverse_intersection[0],
        half_vectors,
        group_fields,
        group_weights[:, None],
        choice,
        origin,
        cholesky,
    )
    own_choice = lax.dynamic_index_in_dim(origin, builder, 0, False)
    kept_weight = lax.dynamic_index_in_dim(grown[:, 0], own_choice, 0, False)
    new_weight = kept_weight * (nb * npr) / overall[0, 0]
    return (stepped[None], new_weight.reshape(1))


def solution(mesh):
    placed = (
        P(None, "build", None),
        P(None, "build", None),
        P(("build", "prop"), None, None),
        P(("build", "prop"), None, None),
        P(),
        P(),
        P(),
    )
    return jax.shard_map(
        shards,
        mesh=mesh,
        in_specs=placed,
        out_specs=(P(("build", "prop"), None, None), P(("build", "prop"))),
        check_vma=False,
    )
```

```python
import functools

import jax
import jax.numpy as jnp
from jax import lax
from jax.experimental import pallas as pl
from jax.experimental.pallas import tpu as pltpu
from jax.sharding import PartitionSpec as P

ORDER = 6
TILE = 16
SLOTS = 4
MESH = pl.DeviceIdType.MESH
f32 = jnp.float32
bf16 = jnp.bfloat16


def spread(coeffs, wide):
    count, vectors = coeffs.shape
    lane = lax.broadcasted_iota(jnp.int32, (vectors, wide), 1) // TILE
    row = lax.broadcasted_iota(jnp.int32, (vectors, wide), 0)
    repeat_columns = (lane == row).astype(f32).astype(bf16)
    line = lax.broadcasted_iota(jnp.int32, (count * TILE, count), 0) // TILE
    walker = lax.broadcasted_iota(jnp.int32, (count * TILE, count), 1)
    repeat_rows = (line == walker).astype(f32).astype(bf16)
    along = jnp.dot(coeffs, repeat_columns, preferred_element_type=f32).astype(bf16)
    both = jnp.dot(repeat_rows, along, preferred_element_type=f32)
    at_row = lax.broadcasted_iota(jnp.int32, (count * TILE, wide), 0) % TILE
    at_lane = lax.broadcasted_iota(jnp.int32, (count * TILE, wide), 1) % TILE
    return jnp.where(at_row == at_lane, both, 0.0).astype(bf16)


def step_kernel(
    nb,
    npr,
    walker_ref,
    inverse_ref,
    half_ref,
    fields_ref,
    weights_ref,
    origin_ref,
    chol_ref,
    out_ref,
    fresh_ref,
    drawn_ref,
    heavy_ref,
    coeffs_ref,
    grown_ref,
    got,
    inverses,
    theta,
    mixed,
    parts,
    sums,
    picked_ref,
    starts_ref,
    chunks,
    mixer,
    tiles,
    pot,
    terms,
    summed,
    partial,
    finals,
    landed,
    load_sem,
    self_sem,
    got_send,
    got_recv,
    inverse_send,
    inverse_recv,
    part_send,
    part_recv,
    sum_send,
    sum_recv,
    pot_send,
    pot_recv,
    state_send,
    state_recv,
    term_send,
    term_recv,
    last_send,
    last_recv,
):
    me = lax.axis_index("build")
    mine = lax.axis_index("prop")
    nh = nb // 2
    half = me // nh
    place = lax.rem(me, nh)
    peer = lax.rem(me + nh, nb)
    vectors, br, orbitals = chol_ref.shape
    electrons = walker_ref.shape[1]
    wide = vectors * TILE
    lanes = parts.shape[2]
    hr = orbitals // 2
    row_tiles = br // TILE
    slots = chunks.shape[0]
    group = min(nb, 8)
    cols = min(orbitals, 512)
    rows = min(hr, 512)
    pieces = min(4, row_tiles)

    def load(t):
        slot = lax.rem(t, slots)
        return pltpu.make_async_copy(
            chol_ref.at[:, pl.ds(t * TILE, TILE), :], chunks.at[slot], load_sem.at[slot]
        )

    def others(ref, sem, count):
        return pltpu.make_async_copy(ref.at[pl.ds(0, count)], ref.at[pl.ds(0, count)], sem)

    barrier = pltpu.get_barrier_semaphore()

    def greet(j, carry):
        pl.semaphore_signal(
            barrier, inc=1, device_id={"build": lax.rem(me + j, nb)}, device_id_type=MESH
        )
        return carry

    lax.fori_loop(1, nb, greet, 0)
    for j in range(1, npr):
        pl.semaphore_signal(
            barrier, inc=1, device_id={"prop": lax.rem(mine + j, npr)}, device_id_type=MESH
        )
    for t in range(min(slots, row_tiles)):
        load(jnp.int32(t)).start()
    own_rows = pl.ds(pl.multiple_of(me * br, br), br)
    got[me] = walker_ref[own_rows, :]
    inverses[me] = inverse_ref[...]

    def collect(v, carry):
        drawn_ref[pl.ds(v, 1), :] = fields_ref[pl.ds(v * npr + mine, 1), :]
        heavy_ref[pl.ds(v, 1), :] = jnp.full((1, 128), weights_ref[v * npr + mine], f32)
        return carry

    lax.fori_loop(0, nb, collect, 0)
    pl.semaphore_wait(barrier, nb - 1 + npr - 1)

    def share(j, carry):
        to = lax.rem(me + j, nb)
        pltpu.make_async_remote_copy(
            src_ref=inverse_ref,
            dst_ref=inverses.at[me],
            send_sem=inverse_send,
            recv_sem=inverse_recv,
            device_id={"build": to},
            device_id_type=MESH,
        ).start()
        pltpu.make_async_remote_copy(
            src_ref=walker_ref.at[pl.ds(to * br, br)],
            dst_ref=got.at[me],
            send_sem=got_send,
            recv_sem=got_recv,
            device_id={"build": to},
            device_id_type=MESH,
        ).start()
        return carry

    lax.fori_loop(1, nb, share, 0)
    others(inverses, inverse_recv, nb - 1).wait()
    others(got, got_recv, nb - 1).wait()

    def rotate(v, carry):
        theta[v] = jnp.dot(got[v], inverses[v], preferred_element_type=f32).astype(bf16)
        starts_ref[v] = got[lax.div(origin_ref[v * npr + mine], npr)]
        return carry

    lax.fori_loop(0, nb, rotate, 0)

    def bias(u, carry):
        first = pl.multiple_of(u * group, group)
        mixed[...] = jnp.zeros_like(mixed)

        def add(t, inner):
            at = pl.ds(pl.multiple_of(t * TILE, TILE), TILE)
            left = theta[pl.ds(first, group), at, :].reshape(group * TILE, electrons)
            right = half_ref[:, at, :].reshape(wide, electrons)
            mixed[...] += lax.dot_general(
                left, right, (((1,), (1,)), ((), ())), preferred_element_type=f32
            )
            return inner

        lax.fori_loop(0, row_tiles, add, 0)
        at_row = lax.broadcasted_iota(jnp.int32, (group * TILE, wide), 0) % TILE
        at_lane = lax.broadcasted_iota(jnp.int32, (group * TILE, wide), 1) % TILE
        kept = jnp.where(at_row == at_lane, mixed[...], 0.0)
        short = jnp.sum(kept.reshape(group, TILE, wide), axis=1)
        source = lax.broadcasted_iota(jnp.int32, (wide, lanes), 0) // TILE
        target = lax.broadcasted_iota(jnp.int32, (wide, lanes), 1)
        gather = (source == target).astype(f32)
        parts[me, pl.ds(first, group), :] = jnp.dot(
            short, gather, precision=lax.Precision.HIGHEST, preferred_element_type=f32
        )
        return carry

    lax.fori_loop(0, nb // group, bias, 0)

    def tell(j, carry):
        pltpu.make_async_remote_copy(
            src_ref=parts.at[me],
            dst_ref=parts.at[me],
            send_sem=part_send,
            recv_sem=part_recv,
            device_id={"build": lax.rem(me + j, nb)},
            device_id_type=MESH,
        ).start()
        return carry

    lax.fori_loop(1, nb, tell, 0)

    def send_state(s, j):
        to = lax.rem(me + j, nb)
        return pltpu.make_async_remote_copy(
            src_ref=starts_ref.at[lax.rem(to, nh) + s * nh],
            dst_ref=terms.at[0, s, own_rows],
            send_sem=state_send.at[s],
            recv_sem=state_recv.at[s],
            device_id={"build": to},
            device_id_type=MESH,
        )

    def push_states(s):
        def push_state(j, carry):
            send_state(s, j).start()
            return carry

        lax.fori_loop(1, nb, push_state, 0)

    push_states(0)
    for s in range(2):
        terms[0, s, own_rows, :] = starts_ref[place + s * nh]
    others(parts, part_recv, nb - 1).wait()
    force_bias = lax.fori_loop(
        1, nb, lambda j, held: held + parts[j], parts[0]
    )
    force_bias = force_bias[:, :vectors]
    drawn = drawn_ref[...]
    exponent = jnp.sum(force_bias * (drawn - 0.5 * force_bias), axis=-1, keepdims=True)
    grown = heavy_ref[...] * jnp.exp(exponent)
    grown_ref[...] = grown
    sums[mine] = jnp.broadcast_to(jnp.sum(grown, axis=0, keepdims=True), sums.shape[1:])
    for j in range(1, npr):
        pltpu.make_async_remote_copy(
            src_ref=sums.at[mine],
            dst_ref=sums.at[mine],
            send_sem=sum_send,
            recv_sem=sum_recv,
            device_id={"prop": lax.rem(mine + j, npr)},
            device_id_type=MESH,
        ).start()
    coeffs_ref[...] = drawn - force_bias

    def pick(v, carry):
        picked_ref[pl.ds(v, 1), :] = coeffs_ref[pl.ds(lax.div(origin_ref[v * npr + mine], npr), 1), :]
        return carry

    lax.fori_loop(0, nb, pick, 0)

    def fill(v, carry):
        c = picked_ref[pl.ds(pl.multiple_of(v * group, group), group), :].astype(bf16)
        at = pl.ds(pl.multiple_of(v * group * TILE, group * TILE), group * TILE)
        mixer[at, :] = spread(c, wide)
        return carry

    if nb == group:
        mixer[...] = spread(picked_ref[...].astype(bf16), wide)
    else:
        lax.fori_loop(0, nb // group, fill, 0)

    def send_pot(s, j, first, count):
        to = lax.rem(place + j, nh)
        return pltpu.make_async_remote_copy(
            src_ref=tiles.at[to + s * nh, pl.ds(first, count)],
            dst_ref=pot.at[s, pl.ds(place * br + first, count)],
            send_sem=pot_send.at[s],
            recv_sem=pot_recv.at[s],
            device_id={"build": half * nh + to},
            device_id_type=MESH,
        )

    def block(t, carry):
        slot = lax.rem(t, slots)
        load(t).wait()

        def part(i, inner):
            v = i // (orbitals // cols)
            c = lax.rem(i, orbitals // cols) * cols
            c = pl.multiple_of(c, cols)
            right = chunks[slot, :, :, pl.ds(c, cols)].reshape(vectors * TILE, cols)
            left = mixer[pl.ds(pl.multiple_of(v * group * TILE, group * TILE), group * TILE), :]
            made = jnp.dot(left, right, preferred_element_type=f32).astype(bf16)
            tiles[pl.ds(v * group, group), pl.ds(pl.multiple_of(t * TILE, TILE), TILE), pl.ds(c, cols)] = (
                made.reshape(group, TILE, cols)
            )
            return inner

        lax.fori_loop(0, (nb // group) * (orbitals // cols), part, 0)

        @pl.when(t + slots < row_tiles)
        def _():
            load(t + slots).start()

        def push(j, inner):
            send_pot(0, j, t * TILE, TILE).start()
            return inner

        lax.fori_loop(1, nh, push, 0)
        return carry

    lax.fori_loop(0, row_tiles, block, 0)

    push_states(1)

    def keep(s):
        return pltpu.make_async_copy(
            tiles.at[place + s * nh], pot.at[s, pl.ds(place * br, br)], self_sem.at[s]
        )

    for s in range(2):
        keep(s).start()

    far = (nh - 1) * br

    def push_rest(piece):
        count = br // pieces

        def push_one(j, carry):
            send_pot(1, j, piece * count, count).start()
            return carry

        lax.fori_loop(1, nh, push_one, 0)

    def send_term(k, s, first):
        at = pl.ds(half * hr + first, rows)
        return pltpu.make_async_remote_copy(
            src_ref=terms.at[k, s, at],
            dst_ref=terms.at[k, s, at],
            send_sem=term_send.at[k, s],
            recv_sem=term_recv.at[k, s],
            device_id={"build": peer},
            device_id_type=MESH,
        )

    def send_last(s, first):
        return pltpu.make_async_remote_copy(
            src_ref=finals.at[s, pl.ds(first, rows)],
            dst_ref=landed.at[pl.ds(first, rows)],
            send_sem=last_send,
            recv_sem=last_recv,
            device_id={"build": peer},
            device_id_type=MESH,
        )

    own_half = pl.ds(pl.multiple_of(half * hr, hr), hr)
    other_half = pl.ds(pl.multiple_of((1 - half) * hr, hr), hr)

    def advance(k, s):
        if k == 1:
            others(terms.at[0, s], state_recv.at[s], (nb - 1) * br).wait()
            keep(s).wait()
            others(pot.at[s], pot_recv.at[s], far).wait()
        else:
            others(terms.at[k - 1, s], term_recv.at[k - 1, s], hr).wait()

        def piece(i, carry):
            first = pl.multiple_of(i * rows, rows)
            at = pl.ds(first, rows)
            here = pl.ds(pl.multiple_of(half * hr + first, rows), rows)
            if k == 1:
                product = jnp.dot(pot[s, at, :], terms[0, s], preferred_element_type=f32)
            else:
                product = partial[s, at, :] + jnp.dot(
                    pot[s, at, other_half], terms[k - 1, s, other_half, :],
                    preferred_element_type=f32,
                )
            product = product / k
            if k == 1:
                total = terms[0, s, here, :].astype(f32) + product
            else:
                total = summed[s, at, :] + product
            if k < ORDER:
                summed[s, at, :] = total
                terms[k, s, here, :] = product.astype(bf16)
                send_term(k, s, first).start()
            else:
                finals[s, at, :] = total.astype(bf16)

                @pl.when(half != s)
                def _():
                    send_last(s, first).start()

            return carry

        lax.fori_loop(0, hr // rows, piece, 0)

        def ahead(i, carry):
            at = pl.ds(pl.multiple_of(i * rows, rows), rows)
            partial[s, at, :] = jnp.dot(
                pot[s, at, own_half], terms[k, s, own_half, :], preferred_element_type=f32
            )
            return carry

        if k < ORDER:
            lax.fori_loop(0, hr // rows, ahead, 0)

    lead = 3
    push_rest(0)
    for k in range(1, lead + 1):
        advance(k, 0)
        if k < pieces:
            push_rest(k)
    for k in range(1, ORDER + 1):
        advance(k, 1)
        if k + lead <= ORDER:
            advance(k + lead, 0)

    out_ref[own_half, :] = finals[half]
    others(landed, last_recv, hr).wait()
    out_ref[other_half, :] = landed[...]
    others(landed, last_send, hr).wait()
    others(sums, sum_recv, npr - 1).wait()
    kept = grown_ref[pl.ds(lax.div(origin_ref[me * npr + mine], npr), 1), :]
    fresh_ref[...] = kept * (nb * npr) / jnp.sum(sums[...], axis=0)[0:1, :]
    others(sums, sum_send, npr - 1).wait()
    others(inverses, inverse_send, nb - 1).wait()
    others(got, got_send, nb - 1).wait()
    others(parts, part_send, nb - 1).wait()
    for s in range(2):
        others(pot.at[s], pot_send.at[s], far).wait()
        others(terms.at[0, s], state_send.at[s], (nb - 1) * br).wait()
        for k in range(1, ORDER):
            others(terms.at[k, s], term_send.at[k, s], hr).wait()


def shards(cholesky, half_vectors, walkers, inverse_intersection, fields, weights, sources):
    nb = lax.axis_size("build")
    npr = lax.axis_size("prop")
    vectors, br, orbitals = cholesky.shape
    electrons = walkers.shape[2]
    hr = orbitals // 2
    wide = vectors * TILE
    lanes = -(-vectors // 128) * 128
    group = min(nb, 8)
    slots = min(SLOTS, br // TILE)
    vmem = pl.BlockSpec(memory_space=pltpu.VMEM)
    dma = pltpu.SemaphoreType.DMA
    stepped, fresh = pl.pallas_call(
        functools.partial(step_kernel, nb, npr),
        out_shape=(
            jax.ShapeDtypeStruct((orbitals, electrons), bf16),
            jax.ShapeDtypeStruct((1, 128), f32),
        ),
        in_specs=[vmem] * 4
        + [pl.BlockSpec(memory_space=pltpu.SMEM)] * 2
        + [pl.BlockSpec(memory_space=pl.ANY)],
        out_specs=(vmem, vmem),
        scratch_shapes=[
            pltpu.VMEM((nb, vectors), f32),
            pltpu.VMEM((nb, 128), f32),
            pltpu.VMEM((nb, vectors), f32),
            pltpu.VMEM((nb, 128), f32),
            pltpu.VMEM((nb, br, electrons), bf16),
            pltpu.VMEM((nb,) + inverse_intersection.shape[1:], bf16),
            pltpu.VMEM((nb, br, electrons), bf16),
            pltpu.VMEM((group * TILE, wide), f32),
            pltpu.VMEM((nb, nb, lanes), f32),
            pltpu.VMEM((npr, 8, 128), f32),
            pltpu.VMEM((nb, vectors), f32),
            pltpu.VMEM((nb, br, electrons), bf16),
            pltpu.VMEM((slots, vectors, TILE, orbitals), bf16),
            pltpu.VMEM((nb * TILE, wide), bf16),
            pltpu.VMEM((nb, br, orbitals), bf16),
            pltpu.VMEM((2, hr, orbitals), bf16),
            pltpu.VMEM((ORDER, 2, orbitals, electrons), bf16),
            pltpu.VMEM((2, hr, electrons), f32),
            pltpu.VMEM((2, hr, electrons), f32),
            pltpu.VMEM((2, hr, electrons), bf16),
            pltpu.VMEM((hr, electrons), bf16),
            dma((slots,)),
            dma((2,)),
            dma,
            dma,
            dma,
            dma,
            dma,
            dma,
            dma,
            dma,
            dma((2,)),
            dma((2,)),
            dma((2,)),
            dma((2,)),
            dma((ORDER, 2)),
            dma((ORDER, 2)),
            dma,
            dma,
        ],
        compiler_params=pltpu.CompilerParams(
            collective_id=0, has_side_effects=True, vmem_limit_bytes=60 * 1024 * 1024
        ),
    )(
        walkers[0],
        inverse_intersection[0],
        half_vectors,
        fields,
        weights,
        sources,
        cholesky,
    )
    return (stepped[None], fresh[0, :1])


def solution(mesh):
    placed = (
        P(None, "build", None),
        P(None, "build", None),
        P(("build", "prop"), None, None),
        P(("build", "prop"), None, None),
        P(),
        P(),
        P(),
    )
    return jax.shard_map(
        shards,
        mesh=mesh,
        in_specs=placed,
        out_specs=(P(("build", "prop"), None, None), P(("build", "prop"))),
        check_vma=False,
    )
```

```python
import functools

import jax
import jax.numpy as jnp
from jax import lax
from jax.experimental import pallas as pl
from jax.experimental.pallas import tpu as pltpu
from jax.sharding import PartitionSpec as P

ORDER = 6
TILE = 16
SLOTS = 4
MESH = pl.DeviceIdType.MESH
f32 = jnp.float32
bf16 = jnp.bfloat16


def spread(coeffs, wide):
    count, vectors = coeffs.shape
    lane = lax.broadcasted_iota(jnp.int32, (vectors, wide), 1) // TILE
    row = lax.broadcasted_iota(jnp.int32, (vectors, wide), 0)
    repeat_columns = (lane == row).astype(f32).astype(bf16)
    line = lax.broadcasted_iota(jnp.int32, (count * TILE, count), 0) // TILE
    walker = lax.broadcasted_iota(jnp.int32, (count * TILE, count), 1)
    repeat_rows = (line == walker).astype(f32).astype(bf16)
    along = jnp.dot(coeffs, repeat_columns, preferred_element_type=f32).astype(bf16)
    both = jnp.dot(repeat_rows, along, preferred_element_type=f32)
    at_row = lax.broadcasted_iota(jnp.int32, (count * TILE, wide), 0) % TILE
    at_lane = lax.broadcasted_iota(jnp.int32, (count * TILE, wide), 1) % TILE
    return jnp.where(at_row == at_lane, both, 0.0).astype(bf16)


def step_kernel(
    nb,
    npr,
    walker_ref,
    inverse_ref,
    half_ref,
    fields_ref,
    weights_ref,
    origin_ref,
    chol_ref,
    out_ref,
    fresh_ref,
    drawn_ref,
    heavy_ref,
    coeffs_ref,
    grown_ref,
    got,
    inverses,
    theta,
    mixed,
    parts,
    sums,
    picked_ref,
    starts_ref,
    chunks,
    mixer,
    tiles,
    pot,
    terms,
    summed,
    partial,
    finals,
    landed,
    load_sem,
    self_sem,
    got_send,
    got_recv,
    inverse_send,
    inverse_recv,
    part_send,
    part_recv,
    sum_send,
    sum_recv,
    pot_send,
    pot_recv,
    state_send,
    state_recv,
    term_send,
    term_recv,
    last_send,
    last_recv,
):
    me = lax.axis_index("build")
    mine = lax.axis_index("prop")
    nh = nb // 2
    half = me // nh
    place = lax.rem(me, nh)
    peer = lax.rem(me + nh, nb)
    vectors, br, orbitals = chol_ref.shape
    electrons = walker_ref.shape[1]
    wide = vectors * TILE
    lanes = parts.shape[2]
    hr = orbitals // 2
    row_tiles = br // TILE
    slots = chunks.shape[0]
    group = min(nb, 8)
    cols = min(orbitals, 512)
    rows = min(hr, 512)
    pieces = min(4, row_tiles)

    def load(t):
        slot = lax.rem(t, slots)
        return pltpu.make_async_copy(
            chol_ref.at[:, pl.ds(t * TILE, TILE), :], chunks.at[slot], load_sem.at[slot]
        )

    def others(ref, sem, count):
        return pltpu.make_async_copy(ref.at[pl.ds(0, count)], ref.at[pl.ds(0, count)], sem)

    barrier = pltpu.get_barrier_semaphore()

    def greet(j, carry):
        pl.semaphore_signal(
            barrier, inc=1, device_id={"build": lax.rem(me + j, nb)}, device_id_type=MESH
        )
        return carry

    lax.fori_loop(1, nb, greet, 0)
    for j in range(1, npr):
        pl.semaphore_signal(
            barrier, inc=1, device_id={"prop": lax.rem(mine + j, npr)}, device_id_type=MESH
        )
    for t in range(min(slots, row_tiles)):
        load(jnp.int32(t)).start()
    own_rows = pl.ds(pl.multiple_of(me * br, br), br)
    got[me] = walker_ref[own_rows, :]
    inverses[me] = inverse_ref[...]

    def collect(v, carry):
        drawn_ref[pl.ds(v, 1), :] = fields_ref[pl.ds(v * npr + mine, 1), :]
        heavy_ref[pl.ds(v, 1), :] = jnp.full((1, 128), weights_ref[v * npr + mine], f32)
        return carry

    lax.fori_loop(0, nb, collect, 0)
    pl.semaphore_wait(barrier, nb - 1 + npr - 1)

    def share(j, carry):
        to = lax.rem(me + j, nb)
        pltpu.make_async_remote_copy(
            src_ref=inverse_ref,
            dst_ref=inverses.at[me],
            send_sem=inverse_send,
            recv_sem=inverse_recv,
            device_id={"build": to},
            device_id_type=MESH,
        ).start()
        pltpu.make_async_remote_copy(
            src_ref=walker_ref.at[pl.ds(to * br, br)],
            dst_ref=got.at[me],
            send_sem=got_send,
            recv_sem=got_recv,
            device_id={"build": to},
            device_id_type=MESH,
        ).start()
        return carry

    lax.fori_loop(1, nb, share, 0)
    others(inverses, inverse_recv, nb - 1).wait()
    others(got, got_recv, nb - 1).wait()

    def rotate(v, carry):
        theta[v] = jnp.dot(got[v], inverses[v], preferred_element_type=f32).astype(bf16)
        starts_ref[v] = got[lax.div(origin_ref[v * npr + mine], npr)]
        return carry

    lax.fori_loop(0, nb, rotate, 0)

    def bias(u, carry):
        first = pl.multiple_of(u * group, group)
        mixed[...] = jnp.zeros_like(mixed)

        def add(t, inner):
            at = pl.ds(pl.multiple_of(t * TILE, TILE), TILE)
            left = theta[pl.ds(first, group), at, :].reshape(group * TILE, electrons)
            right = half_ref[:, at, :].reshape(wide, electrons)
            mixed[...] += lax.dot_general(
                left, right, (((1,), (1,)), ((), ())), preferred_element_type=f32
            )
            return inner

        lax.fori_loop(0, row_tiles, add, 0)
        at_row = lax.broadcasted_iota(jnp.int32, (group * TILE, wide), 0) % TILE
        at_lane = lax.broadcasted_iota(jnp.int32, (group * TILE, wide), 1) % TILE
        kept = jnp.where(at_row == at_lane, mixed[...], 0.0)
        short = jnp.sum(kept.reshape(group, TILE, wide), axis=1)
        source = lax.broadcasted_iota(jnp.int32, (wide, lanes), 0) // TILE
        target = lax.broadcasted_iota(jnp.int32, (wide, lanes), 1)
        gather = (source == target).astype(f32)
        parts[me, pl.ds(first, group), :] = jnp.dot(
            short, gather, precision=lax.Precision.HIGHEST, preferred_element_type=f32
        )
        return carry

    lax.fori_loop(0, nb // group, bias, 0)

    def tell(j, carry):
        pltpu.make_async_remote_copy(
            src_ref=parts.at[me],
            dst_ref=parts.at[me],
            send_sem=part_send,
            recv_sem=part_recv,
            device_id={"build": lax.rem(me + j, nb)},
            device_id_type=MESH,
        ).start()
        return carry

    lax.fori_loop(1, nb, tell, 0)

    def send_state(s, j):
        to = lax.rem(me + j, nb)
        return pltpu.make_async_remote_copy(
            src_ref=starts_ref.at[lax.rem(to, nh) + s * nh],
            dst_ref=terms.at[0, s, own_rows],
            send_sem=state_send.at[s],
            recv_sem=state_recv.at[s],
            device_id={"build": to},
            device_id_type=MESH,
        )

    def push_states(s):
        def push_state(j, carry):
            send_state(s, j).start()
            return carry

        lax.fori_loop(1, nb, push_state, 0)

    push_states(0)
    for s in range(2):
        terms[0, s, own_rows, :] = starts_ref[place + s * nh]
    others(parts, part_recv, nb - 1).wait()
    force_bias = lax.fori_loop(
        1, nb, lambda j, held: held + parts[j], parts[0]
    )
    force_bias = force_bias[:, :vectors]
    drawn = drawn_ref[...]
    exponent = jnp.sum(force_bias * (drawn - 0.5 * force_bias), axis=-1, keepdims=True)
    grown = heavy_ref[...] * jnp.exp(exponent)
    grown_ref[...] = grown
    sums[mine] = jnp.broadcast_to(jnp.sum(grown, axis=0, keepdims=True), sums.shape[1:])
    for j in range(1, npr):
        pltpu.make_async_remote_copy(
            src_ref=sums.at[mine],
            dst_ref=sums.at[mine],
            send_sem=sum_send,
            recv_sem=sum_recv,
            device_id={"prop": lax.rem(mine + j, npr)},
            device_id_type=MESH,
        ).start()
    coeffs_ref[...] = drawn - force_bias

    def pick(v, carry):
        picked_ref[pl.ds(v, 1), :] = coeffs_ref[pl.ds(lax.div(origin_ref[v * npr + mine], npr), 1), :]
        return carry

    lax.fori_loop(0, nb, pick, 0)

    def fill(v, carry):
        c = picked_ref[pl.ds(pl.multiple_of(v * group, group), group), :].astype(bf16)
        at = pl.ds(pl.multiple_of(v * group * TILE, group * TILE), group * TILE)
        mixer[at, :] = spread(c, wide)
        return carry

    if nb == group:
        mixer[...] = spread(picked_ref[...].astype(bf16), wide)
    else:
        lax.fori_loop(0, nb // group, fill, 0)

    def send_pot(s, j, first, count):
        to = lax.rem(place + j, nh)
        return pltpu.make_async_remote_copy(
            src_ref=tiles.at[to + s * nh, pl.ds(first, count)],
            dst_ref=pot.at[s, pl.ds(place * br + first, count)],
            send_sem=pot_send.at[s],
            recv_sem=pot_recv.at[s],
            device_id={"build": half * nh + to},
            device_id_type=MESH,
        )

    def block(t, carry):
        slot = lax.rem(t, slots)
        load(t).wait()

        def part(i, inner):
            v = i // (orbitals // cols)
            c = lax.rem(i, orbitals // cols) * cols
            c = pl.multiple_of(c, cols)
            right = chunks[slot, :, :, pl.ds(c, cols)].reshape(vectors * TILE, cols)
            left = mixer[pl.ds(pl.multiple_of(v * group * TILE, group * TILE), group * TILE), :]
            made = jnp.dot(left, right, preferred_element_type=f32).astype(bf16)
            tiles[pl.ds(v * group, group), pl.ds(pl.multiple_of(t * TILE, TILE), TILE), pl.ds(c, cols)] = (
                made.reshape(group, TILE, cols)
            )
            return inner

        lax.fori_loop(0, (nb // group) * (orbitals // cols), part, 0)

        @pl.when(t + slots < row_tiles)
        def _():
            load(t + slots).start()

        def push(j, inner):
            send_pot(0, j, t * TILE, TILE).start()
            return inner

        lax.fori_loop(1, nh, push, 0)
        return carry

    lax.fori_loop(0, row_tiles, block, 0)

    push_states(1)

    def keep(s):
        return pltpu.make_async_copy(
            tiles.at[place + s * nh], pot.at[s, pl.ds(place * br, br)], self_sem.at[s]
        )

    for s in range(2):
        keep(s).start()

    far = (nh - 1) * br

    def push_rest(piece):
        count = br // pieces

        def push_one(j, carry):
            send_pot(1, j, piece * count, count).start()
            return carry

        lax.fori_loop(1, nh, push_one, 0)

    def send_term(k, s, first):
        at = pl.ds(half * hr + first, rows)
        return pltpu.make_async_remote_copy(
            src_ref=terms.at[k, s, at],
            dst_ref=terms.at[k, s, at],
            send_sem=term_send.at[k, s],
            recv_sem=term_recv.at[k, s],
            device_id={"build": peer},
            device_id_type=MESH,
        )

    def send_last(s, first):
        return pltpu.make_async_remote_copy(
            src_ref=finals.at[s, pl.ds(first, rows)],
            dst_ref=landed.at[pl.ds(first, rows)],
            send_sem=last_send,
            recv_sem=last_recv,
            device_id={"build": peer},
            device_id_type=MESH,
        )

    own_half = pl.ds(pl.multiple_of(half * hr, hr), hr)
    other_half = pl.ds(pl.multiple_of((1 - half) * hr, hr), hr)

    def advance(k, s):
        if k == 1:
            others(terms.at[0, s], state_recv.at[s], (nb - 1) * br).wait()
            keep(s).wait()
            others(pot.at[s], pot_recv.at[s], far).wait()
        else:
            others(terms.at[k - 1, s], term_recv.at[k - 1, s], hr).wait()

        def piece(i, carry):
            first = pl.multiple_of(i * rows, rows)
            at = pl.ds(first, rows)
            here = pl.ds(pl.multiple_of(half * hr + first, rows), rows)
            if k == 1:
                product = jnp.dot(pot[s, at, :], terms[0, s], preferred_element_type=f32)
            else:
                product = partial[s, at, :] + jnp.dot(
                    pot[s, at, other_half], terms[k - 1, s, other_half, :],
                    preferred_element_type=f32,
                )
            product = product / k
            if k == 1:
                total = terms[0, s, here, :].astype(f32) + product
            else:
                total = summed[s, at, :] + product
            if k < ORDER:
                summed[s, at, :] = total
                terms[k, s, here, :] = product.astype(bf16)
                send_term(k, s, first).start()
            else:
                finals[s, at, :] = total.astype(bf16)

                @pl.when(half != s)
                def _():
                    send_last(s, first).start()

            return carry

        lax.fori_loop(0, hr // rows, piece, 0)

        def ahead(i, carry):
            at = pl.ds(pl.multiple_of(i * rows, rows), rows)
            partial[s, at, :] = jnp.dot(
                pot[s, at, own_half], terms[k, s, own_half, :], preferred_element_type=f32
            )
            return carry

        if k < ORDER:
            lax.fori_loop(0, hr // rows, ahead, 0)

    lead = 3
    early = lax.rem(mine, 2) == 1

    @pl.when(early)
    def _():
        for piece in range(pieces):
            push_rest(piece)

    for k in range(1, lead + 1):
        advance(k, 0)

        @pl.when(jnp.logical_not(early))
        def _():
            for piece in range(pieces * (k - 1) // lead, pieces * k // lead):
                push_rest(piece)

    for k in range(1, ORDER + 1):
        advance(k, 1)
        if k + lead <= ORDER:
            advance(k + lead, 0)

    out_ref[own_half, :] = finals[half]
    others(landed, last_recv, hr).wait()
    out_ref[other_half, :] = landed[...]
    others(landed, last_send, hr).wait()
    others(sums, sum_recv, npr - 1).wait()
    kept = grown_ref[pl.ds(lax.div(origin_ref[me * npr + mine], npr), 1), :]
    fresh_ref[...] = kept * (nb * npr) / jnp.sum(sums[...], axis=0)[0:1, :]
    others(sums, sum_send, npr - 1).wait()
    others(inverses, inverse_send, nb - 1).wait()
    others(got, got_send, nb - 1).wait()
    others(parts, part_send, nb - 1).wait()
    for s in range(2):
        others(pot.at[s], pot_send.at[s], far).wait()
        others(terms.at[0, s], state_send.at[s], (nb - 1) * br).wait()
        for k in range(1, ORDER):
            others(terms.at[k, s], term_send.at[k, s], hr).wait()


def shards(cholesky, half_vectors, walkers, inverse_intersection, fields, weights, sources):
    nb = lax.axis_size("build")
    npr = lax.axis_size("prop")
    vectors, br, orbitals = cholesky.shape
    electrons = walkers.shape[2]
    hr = orbitals // 2
    wide = vectors * TILE
    lanes = -(-vectors // 128) * 128
    group = min(nb, 8)
    slots = min(SLOTS, br // TILE)
    vmem = pl.BlockSpec(memory_space=pltpu.VMEM)
    dma = pltpu.SemaphoreType.DMA
    stepped, fresh = pl.pallas_call(
        functools.partial(step_kernel, nb, npr),
        out_shape=(
            jax.ShapeDtypeStruct((orbitals, electrons), bf16),
            jax.ShapeDtypeStruct((1, 128), f32),
        ),
        in_specs=[vmem] * 4
        + [pl.BlockSpec(memory_space=pltpu.SMEM)] * 2
        + [pl.BlockSpec(memory_space=pl.ANY)],
        out_specs=(vmem, vmem),
        scratch_shapes=[
            pltpu.VMEM((nb, vectors), f32),
            pltpu.VMEM((nb, 128), f32),
            pltpu.VMEM((nb, vectors), f32),
            pltpu.VMEM((nb, 128), f32),
            pltpu.VMEM((nb, br, electrons), bf16),
            pltpu.VMEM((nb,) + inverse_intersection.shape[1:], bf16),
            pltpu.VMEM((nb, br, electrons), bf16),
            pltpu.VMEM((group * TILE, wide), f32),
            pltpu.VMEM((nb, nb, lanes), f32),
            pltpu.VMEM((npr, 8, 128), f32),
            pltpu.VMEM((nb, vectors), f32),
            pltpu.VMEM((nb, br, electrons), bf16),
            pltpu.VMEM((slots, vectors, TILE, orbitals), bf16),
            pltpu.VMEM((nb * TILE, wide), bf16),
            pltpu.VMEM((nb, br, orbitals), bf16),
            pltpu.VMEM((2, hr, orbitals), bf16),
            pltpu.VMEM((ORDER, 2, orbitals, electrons), bf16),
            pltpu.VMEM((2, hr, electrons), f32),
            pltpu.VMEM((2, hr, electrons), f32),
            pltpu.VMEM((2, hr, electrons), bf16),
            pltpu.VMEM((hr, electrons), bf16),
            dma((slots,)),
            dma((2,)),
            dma,
            dma,
            dma,
            dma,
            dma,
            dma,
            dma,
            dma,
            dma((2,)),
            dma((2,)),
            dma((2,)),
            dma((2,)),
            dma((ORDER, 2)),
            dma((ORDER, 2)),
            dma,
            dma,
        ],
        compiler_params=pltpu.CompilerParams(
            collective_id=0, has_side_effects=True, vmem_limit_bytes=60 * 1024 * 1024
        ),
    )(
        walkers[0],
        inverse_intersection[0],
        half_vectors,
        fields,
        weights,
        sources,
        cholesky,
    )
    return (stepped[None], fresh[0, :1])


def solution(mesh):
    placed = (
        P(None, "build", None),
        P(None, "build", None),
        P(("build", "prop"), None, None),
        P(("build", "prop"), None, None),
        P(),
        P(),
        P(),
    )
    return jax.shard_map(
        shards,
        mesh=mesh,
        in_specs=placed,
        out_specs=(P(("build", "prop"), None, None), P(("build", "prop"))),
        check_vma=False,
    )
```
